256 devices in a mesh: out: 8 (over x, y_hi), ap: 32 (over z, y_lo, core).
Axes of the slice: x: 4, y: 4 (y_hi: 2, y_lo: 2; y = y_hi * 2 + y_lo), z: 8, core: 2. Of those that a mesh axis runs over, the one named last changes fastest.
Arguments:
- panels: bfloat16 [1280, 256, 2, 1152], P('ap', 'out'), may hold values from -6 to 6
- shot_data: bfloat16 [16, 1280, 2, 1152], P('out', 'ap'), may hold values from -6 to 6
- taper_table: float32 [8, 32], replicated, may hold values from 0.2 to 1
- destination: int32 [8, 1280], P('out', 'ap'), may hold values from -1 to 31, as said below
- taper_level: int32 [8, 1280], P('out', 'ap'), may hold values from 0 to 7
- shot_order: int32 [4], replicated, may hold values from 0 to 15
Outputs:
- multiples: float32 [4, 256, 2, 1152], P(None, 'out', None, 'ap')
The draws below stay inside these ranges and needn't reach their ends.
Inputs may be any that keep to these rules, and one draw needn't show every extreme that they name: For each batch, every index of ap is the destination of exactly 14 locations; the 40 locations stored at one index of ap send at most 2 to any one destination, and at some index all 40 are inside the aperture.
All inputs are finite; a program needn't handle non-finite values.
Results may differ from the reference program's by a relative error of at most 0.0003.
Values may be sent and summed in bfloat16 or wider, within the bound.
A program may use at most 128 MiB of HBM per device.

```python
import jax
import jax.numpy as jnp
from jax import lax

F = 1152
PANEL = 32
K_DEV = 40
LEVELS = 8
SHOTS = 4
NK = 1280
REC = 256
NSRC = 16
N_OUT = 8
N_AP = 32


def route_batch(batch_key):
    patterns = jnp.array([[20, 5, 2, 1], [20, 6, 1, 1], [20, 3, 3, 2]], dtype=jnp.int32)
    keys = jax.random.split(batch_key, 4)
    groups = jax.random.randint(keys[0], (N_AP // 4,), 0, 3)
    counts = patterns[groups].reshape(N_AP)
    holders = jax.random.permutation(keys[1], N_AP)
    counts = counts[holders]
    starts = jnp.cumsum(counts) - counts
    slot_keys = jax.random.split(keys[2], N_AP)

    def shuffle(slot_key):
        return jax.random.permutation(slot_key, K_DEV)
    shuffled = jax.vmap(shuffle)(slot_keys)
    ranks = jnp.argsort(shuffled, axis=1, stable=True).astype(jnp.int32)
    offset = jax.random.randint(keys[3], (), 0, N_AP)
    pairs = starts[:, None] + ranks // 2
    owners = (pairs + offset) % N_AP
    live = ranks < 2 * counts[:, None]
    return jnp.where(live, owners, -1).reshape(N_AP * K_DEV).astype(jnp.int32)


def draw_destination(key, part):
    key = jax.random.fold_in(key, 11)
    return jax.vmap(route_batch)(jax.random.split(key, N_OUT))


def place_ends(values, rng, least, top_value):
    spot = [jax.random.randint(jax.random.fold_in(rng, axis), (), 0, length) for axis, length in enumerate(values.shape)]
    widest = values.shape.index(max(values.shape))
    neighbour = spot[:widest] + [(spot[widest] + 1) % values.shape[widest]] + spot[widest + 1:]
    return values.at[tuple(spot)].set(least).at[tuple(neighbour)].set(top_value)


def shard_levels(rng, shape, cuts, least, largest):
    def one(position, parts):
        draws = jax.random.uniform(jax.random.fold_in(jax.random.fold_in(rng, 6), position), (parts,), jnp.float32, least / len(cuts), largest / len(cuts))
        return jnp.repeat(jnp.exp(draws), shape[position] // parts).reshape((-1,) + (1,) * (len(shape) - position - 1))

    factor_of = one(*cuts[0])
    for cut in cuts[1:]:
        factor_of = factor_of * one(*cut)
    return factor_of


def bell_draw(key, shape, width, reach, cuts=(), kind=jnp.bfloat16):
    values = jax.random.normal(key, shape, jnp.float32) * width
    if len(cuts) > 0:
        values = shard_levels(key, shape, cuts, -0.22, 0.18) * values
    return jnp.clip(values, min=-reach, max=reach).astype(kind)


def setup_inputs(seed: int = 0) -> dict:
    key_list = jax.random.split(jax.random.key(seed), 7)
    panels = bell_draw(key_list[0], (NK, REC, 2, F), 1.0, 6.0, ((0, 32), (1, 8)))
    shot_data = bell_draw(key_list[1], (NSRC, NK, 2, F), 1.0, 6.0, ((0, 8), (1, 32)))
    taper_table = jnp.clip(jax.random.uniform(key_list[2], (LEVELS, PANEL), jnp.float32, 0.2, 1.0), 0.2, 1.0)
    destination = draw_destination(jax.random.fold_in(key_list[6], 71), 0)
    taper_level = place_ends(jax.random.randint(key_list[4], (N_OUT, NK), 0, LEVELS), jax.random.fold_in(key_list[4], 1), 0, LEVELS - 1).astype(jnp.int32)
    shot_order = place_ends(jax.random.randint(key_list[5], (SHOTS,), 0, NSRC), jax.random.fold_in(key_list[5], 1), 0, NSRC - 1).astype(jnp.int32)
    return dict(panels=panels, shot_data=shot_data, taper_table=taper_table, destination=destination, taper_level=taper_level, shot_order=shot_order)


def taper_weights(taper_table, levels):
    count = taper_table.shape[0]
    onehot = (levels[:, None] == jnp.arange(count, dtype=jnp.int32)[None, :]).astype(taper_table.dtype)
    return jnp.dot(onehot, taper_table, precision=lax.Precision.HIGHEST)


def predicted(weights, traces, block):
    real_trace = traces[:, 0, :].astype(jnp.float32)[:, None, :]
    imag_trace = traces[:, 1, :].astype(jnp.float32)[:, None, :]
    real_panel = block[:, :, 0, :].astype(jnp.float32)
    imag_panel = block[:, :, 1, :].astype(jnp.float32)
    scale = weights.astype(jnp.float32)[:, :, None]
    real_part = jnp.sum(scale * (real_trace * real_panel - imag_trace * imag_panel), axis=0)
    imag_part = jnp.sum(scale * (real_trace * imag_panel + imag_trace * real_panel), axis=0)
    return jnp.stack([real_part, imag_part], axis=1)


def reference(panels, shot_data, taper_table, destination, taper_level, shot_order):
    results = []
    for step in range(SHOTS):
        gather_now = lax.dynamic_index_in_dim(shot_data, shot_order[step], 0, keepdims=False)
        batches = []
        for batch in range(N_OUT):
            levels = jnp.where(destination[batch] >= 0, taper_level[batch], -1).astype(jnp.int32)
            weights = taper_weights(taper_table, levels)
            block = panels[:, batch * PANEL:(batch + 1) * PANEL]

            def accumulate(index, total, weights=weights, block=block, gather_now=gather_now):
                start = (index * K_DEV).astype(jnp.int32)
                part_weights = lax.dynamic_slice_in_dim(weights, start, K_DEV, 0)
                part_traces = lax.dynamic_slice_in_dim(gather_now, start, K_DEV, 0)
                part_block = lax.dynamic_slice_in_dim(block, start, K_DEV, 0)
                return total + predicted(part_weights, part_traces, part_block)

            batches.append(lax.fori_loop(0, N_AP, accumulate, jnp.zeros((PANEL, 2, F), jnp.float32)))
        results.append(jnp.concatenate(batches, axis=0))
    return jnp.stack(results, axis=0)
```

```python
import functools

import jax
import jax.numpy as jnp
from jax import lax
from jax.experimental import pallas as pl
from jax.experimental.pallas import tpu as pltpu
from jax.sharding import PartitionSpec as P

F32 = jnp.float32
BF16 = jnp.bfloat16
MESH = pl.DeviceIdType.MESH

F = 1152
R = 32
K = 40
S = 4
N_OUT = 8
CH = K // N_OUT
TILE = 128
MAIN = 1024
LAST = F - MAIN
FB = 36
UNROLL = 8

OUT_OFF = ((1, 1), (3, 1), (2, 1), (1, 0), (3, 0), (2, 0), (0, 1))
Z_OFF = (4, 3, 5, 2, 6, 1, 7)


def kernel(
    panels, shots, table, dest, level, order, out,
    pm, pt, pmf, ptf, wt, recv1, gath, tr, trs, u, v, ts, cs, cr, yr, zr, fs,
    psem, ptsem, own_sem, s1, r1, s2, r2, sc, rc, sy, ry, sz, rz,
):
    o = lax.axis_index("out")
    a = lax.axis_index("ap")
    x, yh = o // 2, o % 2
    z, yl, c = a // 4, (a // 2) % 2, a % 2

    pm_copy = pltpu.make_async_copy(panels.at[:, :, :, pl.ds(0, MAIN)], pm, psem)
    pm_copy.start()
    pt_copies = []
    for r in range(R):
        cp = pltpu.make_async_copy(
            panels.at[:, r, :, pl.ds(MAIN, LAST)], pt.at[:, :, pl.ds(r * LAST, LAST)], ptsem.at[r]
        )
        cp.start()
        pt_copies.append(cp)
    own = pltpu.make_async_copy(shots.at[:, pl.ds(o * CH, CH)], recv1.at[pl.ds(2 * o, 2)], own_sem)
    own.start()

    out_ids = [((lax.rem(x + dx, 4) * 2 + lax.rem(yh + dy, 2)), a) for dx, dy in OUT_OFF]
    core_id = (o, (z * 2 + yl) * 2 + 1 - c)
    y_id = (o, (z * 2 + 1 - yl) * 2 + c)
    z_at = [lax.rem(z + dz, 8) for dz in Z_OFF]
    z_ids = [(o, (zz * 2 + yl) * 2 + c) for zz in z_at]

    barrier = pltpu.get_barrier_semaphore()
    peers = out_ids + [core_id, y_id] + z_ids
    for peer in peers:
        pl.semaphore_signal(barrier, inc=1, device_id=peer, device_id_type=MESH)
    pl.semaphore_wait(barrier, len(peers))

    first = []
    for i, peer in enumerate(out_ids):
        cp = pltpu.make_async_remote_copy(
            src_ref=shots.at[:, pl.ds(peer[0] * CH, CH)], dst_ref=recv1.at[pl.ds(2 * o, 2)],
            send_sem=s1.at[i], recv_sem=r1.at[i], device_id=peer, device_id_type=MESH,
        )
        cp.start()
        first.append(cp)

    def fill(l, _):
        for r in range(R):
            wt[l, :, r * LAST:(r + 1) * LAST] = jnp.full((2, LAST), table[l, r], F32)
        return 0

    lax.fori_loop(0, 8, fill, 0)
    pm_copy.wait()
    for cp in pt_copies:
        cp.wait()

    def weigh(k, _):
        lev = level[0, k]
        live = jnp.where(dest[0, k] >= 0, 1.0, 0.0).astype(F32)
        for r in range(R):
            pmf[k, r] = pm[k, r].astype(F32) * (table[lev, r] * live)
        ptf[k] = pt[k].astype(F32) * (wt[lev] * live)
        return 0

    lax.fori_loop(0, K, weigh, 0)

    own.wait()
    for cp in first:
        cp.wait_recv()

    second = []
    mine = pl.ds(o * CH, CH)
    for s in range(S):
        gath[s, mine] = recv1[order[s]]
        copies = []
        for i, peer in enumerate(out_ids):
            cp = pltpu.make_async_remote_copy(
                src_ref=gath.at[s, mine], dst_ref=gath.at[s, mine],
                send_sem=s2.at[s, i], recv_sem=r2.at[s, i], device_id=peer, device_id_type=MESH,
            )
            cp.start()
            copies.append(cp)
        second.append(copies)

    zero = jnp.zeros((2, 512), F32)

    def traces(s):
        for cp in second[s]:
            cp.wait_recv()

        def body(k, _):
            t = gath[s, k].astype(F32)
            tr[k, :, 0:F] = t
            for i in range(3):
                tr[k, :, F + i * LAST:F + (i + 1) * LAST] = t[:, MAIN:]
            return 0

        lax.fori_loop(0, K, body, 0, unroll=4)

        def swap(k, _):
            trs[k, 0:1] = tr[k, 1:2]
            trs[k, 1:2] = tr[k, 0:1]
            return 0

        lax.fori_loop(0, K, swap, 0, unroll=4)

    def group(load, col, store):
        def body(k, acc):
            t, w = tr[k, :, col:col + 512], trs[k, :, col:col + 512]
            new = []
            for g in range(8):
                p = load(k, g)
                new.append(acc[2 * g] + t * p)
                new.append(acc[2 * g + 1] + w * p)
            return tuple(new)

        acc = lax.fori_loop(0, K, body, (zero,) * 16, unroll=UNROLL)
        for g in range(8):
            store(g, acc[2 * g], acc[2 * g + 1])

    def products(s, parts):
        for part in parts:
            if part < 8:
                half, first_r = part % 2, (part // 2) * 8
                cols = slice(half * 512, half * 512 + 512)

                def load(k, g, first_r=first_r, cols=cols):
                    return pmf[k, first_r + g, :, cols]

                def store(g, p, q, first_r=first_r, cols=cols):
                    u[s, first_r + g, :, cols] = p
                    v[s, first_r + g, :, cols] = q

                group(load, half * 512, store)
            else:

                def load(k, g):
                    return ptf[k, :, g * 512:g * 512 + 512]

                def store(g, p, q):
                    for i in range(4):
                        u[s, g * 4 + i, :, MAIN:F] = p[:, i * LAST:(i + 1) * LAST]
                        v[s, g * 4 + i, :, MAIN:F] = q[:, i * LAST:(i + 1) * LAST]

                group(load, MAIN, store)

    def turn(h):
        even = lax.broadcasted_iota(jnp.int32, (64, TILE), 0) % 2 == 0
        for ft in range(F // TILE):
            rows = []
            for s in (2 * h, 2 * h + 1):
                cols = slice(ft * TILE, (ft + 1) * TILE)
                p = u[s, :, :, cols].reshape(64, TILE)
                q = v[s, :, :, cols].reshape(64, TILE)
                rows.append(jnp.where(even, p - pltpu.roll(p, 63, 0), q + pltpu.roll(q, 1, 0)))
            ts[ft * TILE:(ft + 1) * TILE] = jnp.concatenate(rows, axis=0).T
        for b in range(32):
            cs[h, b % 2, (b // 2) % 2, b // 4] = ts[b * FB:(b + 1) * FB]

    def remote(src, dst, send, recv, peer):
        cp = pltpu.make_async_remote_copy(
            src_ref=src, dst_ref=dst, send_sem=send, recv_sem=recv, device_id=peer, device_id_type=MESH
        )
        cp.start()
        return cp

    def core_start(h):
        return remote(cs.at[h, 1 - c], cr.at[h], sc.at[h], rc.at[h], core_id)

    def y_start(h, cp):
        cp.wait_recv()
        cr[h] = cr[h] + cs[h, c]
        return remote(cr.at[h, 1 - yl], yr.at[h], sy.at[h], ry.at[h], y_id)

    def z_start(h, cp):
        cp.wait_recv()
        yr[h] = yr[h] + cr[h, yl]
        return [
            remote(yr.at[h, z_at[i]], zr.at[h, i], sz.at[h, i], rz.at[h, i], z_ids[i]) for i in range(7)
        ]

    def finish(h, copies):
        for cp in copies:
            cp.wait_recv()
        total = yr[h, z]
        for i in range(7):
            total = total + zr[h, i]
        fs[h, 0:FB] = total
        flat = fs[h].T
        for i in range(2):
            out[2 * h + i] = flat[64 * i:64 * i + 64, 0:FB]

    for s in (0, 1):
        traces(s)
        products(s, range(9))
    turn(0)
    core0 = core_start(0)
    traces(2)
    products(2, range(5))
    y0 = y_start(0, core0)
    products(2, range(5, 9))
    traces(3)
    products(3, range(9))
    turn(1)
    core1 = core_start(1)
    z0 = z_start(0, y0)
    y1 = y_start(1, core1)
    z1 = z_start(1, y1)
    finish(0, z0)
    finish(1, z1)

    for cp in first + [cp for copies in second for cp in copies] + [core0, y0, core1, y1] + z0 + z1:
        cp.wait_send()


def on_device(panels, shot_data, taper_table, destination, taper_level, shot_order):
    vmem = pltpu.VMEM
    dma = pltpu.SemaphoreType.DMA
    hbm = pl.BlockSpec(memory_space=pl.ANY)
    smem = pl.BlockSpec(memory_space=pltpu.SMEM)
    result = pl.pallas_call(
        kernel,
        out_shape=jax.ShapeDtypeStruct((S, 2 * R, FB), F32),
        in_specs=[hbm, hbm, smem, smem, smem, smem],
        out_specs=pl.BlockSpec(memory_space=vmem),
        scratch_shapes=[
            vmem((K, R, 2, MAIN), BF16),
            vmem((K, 2, R * LAST), BF16),
            vmem((K, R, 2, MAIN), F32),
            vmem((K, 2, R * LAST), F32),
            vmem((8, 2, R * LAST), F32),
            vmem((2 * N_OUT, CH, 2, F), BF16),
            vmem((S, K, 2, F), BF16),
            vmem((K, 2, F + 3 * LAST), F32),
            vmem((K, 2, F + 3 * LAST), F32),
            vmem((S, R, 2, F), F32),
            vmem((S, R, 2, F), F32),
            vmem((F, TILE), F32),
            vmem((2, 2, 2, 8, FB, TILE), F32),
            vmem((2, 2, 8, FB, TILE), F32),
            vmem((2, 8, FB, TILE), F32),
            vmem((2, 7, FB, TILE), F32),
            vmem((2, TILE, TILE), F32),
            dma, dma((R,)), dma,
            dma((7,)), dma((7,)), dma((S, 7)), dma((S, 7)),
            dma((2,)), dma((2,)), dma((2,)), dma((2,)), dma((2, 7)), dma((2, 7)),
        ],
        compiler_params=pltpu.CompilerParams(
            collective_id=0, has_side_effects=True, vmem_limit_bytes=48 * 2**20
        ),
        name="multiples",
    )(panels, shot_data, taper_table, destination, taper_level, shot_order)
    return result.reshape(S, R, 2, FB)


def solution(mesh):
    placed = (
        P("ap", "out", None, None),
        P("out", "ap", None, None),
        P(),
        P("out", "ap"),
        P("out", "ap"),
        P(),
    )
    return jax.shard_map(
        on_device, mesh=mesh, in_specs=placed, out_specs=P(None, "out", None, "ap"), check_vma=False
    )
```

```python
import functools

import jax
import jax.numpy as jnp
from jax import lax
from jax.experimental import pallas as pl
from jax.experimental.pallas import tpu as pltpu
from jax.sharding import PartitionSpec as P

F32 = jnp.float32
BF16 = jnp.bfloat16
MESH = pl.DeviceIdType.MESH

F = 1152
R = 32
K = 40
S = 4
N_OUT = 8
CH = K // N_OUT
TILE = 128
MAIN = 1024
LAST = F - MAIN
FB = 36
HB = FB // 2
UNROLL = 8

OUT_OFF = ((1, 1), (3, 1), (2, 1), (1, 0), (3, 0), (2, 0), (0, 1))
X_OFF = (2, 1, 3)
WAYS = ("all", "all", "all", "all")
Z_OFF = (4, 3, 5, 2, 6, 1, 7)


def kernel(
    panels, shots, table_hbm, dest_hbm, level_hbm, order_hbm, out,
    table, dest, level, order,
    pm, pt, tmp, tmpl, pmf, ptf, wt, recv1, gath, tr, xs, xl, ts, cs, cr, ys, yo, yr, zs, zr, fs,
    small_sem, psem, ptsem, own_sem, s1, r1, s2, r2, s2x, r2x, sc, rc, sy, ry, sz, rz,
):
    o = lax.axis_index("out")
    a = lax.axis_index("ap")
    x, yh = o // 2, o % 2
    z, yl, c = a // 4, (a // 2) % 2, a % 2

    small = []
    for i, (src, dst) in enumerate(((table_hbm, table), (dest_hbm, dest), (level_hbm, level), (order_hbm, order))):
        cp = pltpu.make_async_copy(src, dst, small_sem.at[i])
        cp.start()
        small.append(cp)

    pm_copy = pltpu.make_async_copy(panels.at[:, :, :, pl.ds(0, MAIN)], pm, psem)
    pm_copy.start()
    pt_copies = []
    for r in range(R):
        cp = pltpu.make_async_copy(
            panels.at[:, r, :, pl.ds(MAIN, LAST)], pt.at[:, :, pl.ds(r * LAST, LAST)], ptsem.at[r]
        )
        cp.start()
        pt_copies.append(cp)
    own = pltpu.make_async_copy(shots.at[:, pl.ds(o * CH, CH)], recv1.at[pl.ds(2 * o, 2)], own_sem)
    own.start()

    out_ids = [((lax.rem(x + dx, 4) * 2 + lax.rem(yh + dy, 2)), a) for dx, dy in OUT_OFF]
    x_ids = [(lax.rem(x + dx, 4) * 2 + yh, a) for dx in X_OFF]
    row_id = (x * 2 + 1 - yh, a)
    core_id = (o, (z * 2 + yl) * 2 + 1 - c)
    y_id = (o, (z * 2 + 1 - yl) * 2 + c)
    z_at = [lax.rem(z + dz, 8) for dz in Z_OFF]
    z_ids = [(o, (zz * 2 + yl) * 2 + c) for zz in z_at]

    barrier = pltpu.get_barrier_semaphore()
    peers = out_ids + [core_id, y_id] + z_ids
    for peer in peers:
        pl.semaphore_signal(barrier, inc=1, device_id=peer, device_id_type=MESH)
    pl.semaphore_wait(barrier, len(peers))

    first = []
    for i, peer in enumerate(out_ids):
        cp = pltpu.make_async_remote_copy(
            src_ref=shots.at[:, pl.ds(peer[0] * CH, CH)], dst_ref=recv1.at[pl.ds(2 * o, 2)],
            send_sem=s1.at[i], recv_sem=r1.at[i], device_id=peer, device_id_type=MESH,
        )
        cp.start()
        first.append(cp)

    for cp in small:
        cp.wait()

    def fill(l, _):
        for r in range(R):
            wt[l, :, r * LAST:(r + 1) * LAST] = jnp.full((1, LAST), table[l, r], F32)
        return 0

    lax.fori_loop(0, 8, fill, 0)
    pm_copy.wait()
    for cp in pt_copies:
        cp.wait()

    def weigh(k, _):
        lev = level[0, k]
        live = jnp.where(dest[0, k] >= 0, 1.0, 0.0).astype(F32)
        for r in range(R):
            tmp[r] = pm[k, r].astype(F32)
        tmpl[...] = pt[k].astype(F32)
        for r in range(R):
            weight = table[lev, r] * live
            re = tmp[r, 0:1] * weight
            im = tmp[r, 1:2] * weight
            pmf[k, 0, r] = re
            pmf[k, 1, r] = im - re
            pmf[k, 2, r] = re + im
        weight = wt[lev] * live
        re = tmpl[0:1] * weight
        im = tmpl[1:2] * weight
        for i, value in enumerate((re, im - re, re + im)):
            ptf[k, i] = value.reshape(R, LAST)
        return 0

    lax.fori_loop(0, K, weigh, 0)

    own.wait()
    for cp in first:
        cp.wait_recv()

    def remote(src, dst, send, recv, peer):
        cp = pltpu.make_async_remote_copy(
            src_ref=src, dst_ref=dst, send_sem=send, recv_sem=recv, device_id=peer, device_id_type=MESH
        )
        cp.start()
        return cp

    for s in range(S):
        gath[s, x, yh] = recv1[order[s]]

    def spread(s, peers, to, send, recv):
        part = gath.at[(s,) + to]
        return [remote(part, part, send.at[s, i], recv.at[s, i], peer) for i, peer in enumerate(peers)]

    near = []
    for s, way in enumerate(WAYS):
        if way == "all":
            near.append(spread(s, out_ids, (x, yh), s2, r2))
        elif way == "y":
            near.append(spread(s, [row_id], (x, yh), s2, r2))
        else:
            near.append(spread(s, x_ids, (x, yh), s2, r2))
    second = []
    for s, way in enumerate(WAYS):
        if way == "all":
            second.append(near[s])
            continue
        for cp in near[s]:
            cp.wait_recv()
        if way == "y":
            second.append(spread(s, x_ids, (x,), s2x, r2x))
        else:
            second.append(spread(s, [row_id], (slice(None), yh), s2x, r2x))
    rows = [cp for s, way in enumerate(WAYS) if way != "all" for cp in near[s]]

    def traces(s):
        for cp in second[s]:
            cp.wait_recv()

        def body(k, _):
            tr[k] = gath[s, k // (2 * CH), (k // CH) % 2, k % CH].astype(F32)
            return 0

        lax.fori_loop(0, K, body, 0, unroll=4)

    def sums(width, load, cols, count, shape):
        def body(k, acc):
            a, b = tr[k, 0:1, cols], tr[k, 1:2, cols]
            t = (a + b, a, b)
            return tuple(acc[3 * g + i] + t[i] * load(k, i, g) for g in range(count) for i in range(3))

        acc = lax.fori_loop(0, K, body, (jnp.zeros(shape, F32),) * (3 * count), unroll=UNROLL)
        return [(acc[3 * g] - acc[3 * g + 2], acc[3 * g] + acc[3 * g + 1]) for g in range(count)]

    def products(s, parts):
        for part in parts:
            if part < 4:
                pairs = sums(
                    MAIN, lambda k, i, g, part=part: pmf[k, i, part * 8 + g], slice(0, MAIN), 8, (1, MAIN)
                )
                for g, (re, im) in enumerate(pairs):
                    r = part * 8 + g
                    xs[s, 2 * r:2 * r + 1] = re
                    xs[s, 2 * r + 1:2 * r + 2] = im
            else:
                pairs = sums(
                    LAST, lambda k, i, g: ptf[k, i, g * 8:g * 8 + 8], slice(MAIN, F), 4, (8, LAST)
                )
                for g, (re, im) in enumerate(pairs):
                    xl[s, pl.ds(g * 16, 8, stride=2)] = re
                    xl[s, pl.ds(g * 16 + 1, 8, stride=2)] = im

    def turn(s):
        copies = []
        tiles = [xl[s] if ft == 8 else xs[s, :, ft * TILE:(ft + 1) * TILE] for ft in range(F // TILE)]
        turned = [pltpu.roll(tile, TILE // 2, 1) for tile in tiles[4:]]
        low = lax.broadcasted_iota(jnp.int32, (2 * R, TILE), 1) < TILE // 2
        for j in range(5):
            upper = jnp.where(low, turned[j], turned[min(j + 1, 4)])
            ts[j * TILE:(j + 1) * TILE] = jnp.concatenate([tiles[j], upper], axis=0).T
            if j in (2, 4):
                part = j // 4
                for b in range(part * 8, part * 8 + 8):
                    cs[s, b % 2, (b // 2) % 2, b // 4] = ts[b * FB:(b + 1) * FB]
                zz = pl.ds(2 * part, 2)
                copies.append(
                    remote(cs.at[s, 1 - c, :, zz], cr.at[s, :, zz], sc.at[s, part], rc.at[s, part], core_id)
                )
        return copies

    def y_start(s, copies):
        for cp in copies:
            cp.wait_recv()
        ys[s] = cs[s, c, 1 - yl] + cr[s, 1 - yl]
        sent = remote(ys.at[s], yr.at[s], sy.at[s], ry.at[s], y_id)
        yo[s] = cs[s, c, yl] + cr[s, yl]
        return [sent]

    def z_start(s, copies):
        copies[0].wait_recv()
        low = lax.broadcasted_iota(jnp.int32, (HB, TILE), 1) < TILE // 2
        for zz in range(4):
            first_half = yo[s, zz, 0:HB] + yr[s, zz, 0:HB]
            second_half = yo[s, zz, HB:FB] + yr[s, zz, HB:FB]
            zs[s, zz] = jnp.where(low, first_half, pltpu.roll(second_half, TILE // 2, 1))
            zs[s, zz + 4] = jnp.where(low, pltpu.roll(first_half, TILE // 2, 1), second_half)
        return [remote(zs.at[s, z_at[i]], zr.at[s, i], sz.at[s, i], rz.at[s, i], z_ids[i]) for i in range(7)]

    def finish(s, copies):
        for cp in copies:
            cp.wait_recv()
        total = zs[s, z]
        for i in range(7):
            total = total + zr[s, i]
        fs[s, 0:HB] = total
        flat = fs[s].T
        out[s, :, 0:HB] = flat[0:2 * R, 0:HB]
        out[s, :, HB:FB] = flat[2 * R:, 0:HB]

    traces(0)
    products(0, range(5))
    core = [turn(0)]
    traces(1)
    products(1, range(3))
    y = [y_start(0, core[0])]
    products(1, range(3, 5))
    core.append(turn(1))
    traces(2)
    products(2, range(3))
    y.append(y_start(1, core[1]))
    products(2, range(3, 5))
    core.append(turn(2))
    traces(3)
    products(3, range(3))
    y.append(y_start(2, core[2]))
    zc = [z_start(0, y[0])]
    products(3, range(3, 5))
    core.append(turn(3))
    zc.append(z_start(1, y[1]))
    y.append(y_start(3, core[3]))
    zc.append(z_start(2, y[2]))
    zc.append(z_start(3, y[3]))
    for s in range(S):
        finish(s, zc[s])

    for cp in first + rows + [cp for copies in second + core + y + zc for cp in copies]:
        cp.wait_send()


def on_device(panels, shot_data, taper_table, destination, taper_level, shot_order):
    vmem = pltpu.VMEM
    dma = pltpu.SemaphoreType.DMA
    hbm = pl.BlockSpec(memory_space=pltpu.HBM)
    result = pl.pallas_call(
        kernel,
        out_shape=jax.ShapeDtypeStruct((S, 2 * R, FB), F32),
        in_specs=[hbm] * 6,
        out_specs=pl.BlockSpec(memory_space=vmem),
        scratch_shapes=[
            pltpu.SMEM((8, R), F32),
            pltpu.SMEM((1, K), jnp.int32),
            pltpu.SMEM((1, K), jnp.int32),
            pltpu.SMEM((S,), jnp.int32),
            vmem((K, R, 2, MAIN), BF16),
            vmem((K, 2, R * LAST), BF16),
            vmem((R, 2, MAIN), F32),
            vmem((2, R * LAST), F32),
            vmem((K, 3, R, 1, MAIN), F32),
            vmem((K, 3, R, LAST), F32),
            vmem((8, 1, R * LAST), F32),
            vmem((2 * N_OUT, CH, 2, F), BF16),
            vmem((S, 4, 2, CH, 2, F), BF16),
            vmem((K, 2, F), F32),
            vmem((S, 2 * R, MAIN), F32),
            vmem((S, 2 * R, LAST), F32),
            vmem((5 * TILE, TILE), F32),
            vmem((S, 2, 2, 4, FB, TILE), F32),
            vmem((S, 2, 4, FB, TILE), F32),
            vmem((S, 4, FB, TILE), F32),
            vmem((S, 4, FB, TILE), F32),
            vmem((S, 4, FB, TILE), F32),
            vmem((S, 8, HB, TILE), F32),
            vmem((S, 7, HB, TILE), F32),
            vmem((S, TILE, TILE), F32),
            dma((4,)), dma, dma((R,)), dma,
            dma((7,)), dma((7,)), dma((S, 7)), dma((S, 7)), dma((S, 3)), dma((S, 3)),
            dma((S, 2)), dma((S, 2)), dma((S,)), dma((S,)), dma((S, 7)), dma((S, 7)),
        ],
        compiler_params=pltpu.CompilerParams(
            collective_id=0, has_side_effects=True, vmem_limit_bytes=48 * 2**20
        ),
        name="multiples",
    )(*[pltpu.with_memory_space_constraint(v, pltpu.HBM) for v in (panels, shot_data, taper_table, destination, taper_level, shot_order)])
    return result.reshape(S, R, 2, FB)


def solution(mesh):
    placed = (
        P("ap", "out", None, None),
        P("out", "ap", None, None),
        P(),
        P("out", "ap"),
        P("out", "ap"),
        P(),
    )
    return jax.shard_map(
        on_device, mesh=mesh, in_specs=placed, out_specs=P(None, "out", None, "ap"), check_vma=False
    )
```

```python
import functools

import jax
import jax.numpy as jnp
from jax import lax
from jax.experimental import pallas as pl
from jax.experimental.pallas import tpu as pltpu
from jax.sharding import PartitionSpec as P

F32 = jnp.float32
BF16 = jnp.bfloat16
MESH = pl.DeviceIdType.MESH

F = 1152
R = 32
K = 40
S = 4
N_OUT = 8
CH = K // N_OUT
TILE = 128
MAIN = 1024
LAST = F - MAIN
FB = 36
HB = FB // 2
UNROLL = 20

OUT_OFF = ((1, 1), (3, 1), (2, 1), (1, 0), (3, 0), (2, 0), (0, 1))
Z_OFF = (4, 3, 5, 2, 6, 1, 7)


def kernel(
    panels, shots, table_hbm, dest_hbm, level_hbm, order_hbm, out,
    table, dest, level, order,
    pm, pt, tmp, tmpl, pmf, ptf, wt, recv1, gath, tr, xs, xl, ts, cs, cr, ys, yo, yr, zs, zr, fs,
    small_sem, psem, ptsem, own_sem, s1, r1, s2, r2, sc, rc, sy, ry, sz, rz,
):
    o = lax.axis_index("out")
    a = lax.axis_index("ap")
    x, yh = o // 2, o % 2
    z, yl, c = a // 4, (a // 2) % 2, a % 2

    small = []
    for i, (src, dst) in enumerate(((table_hbm, table), (dest_hbm, dest), (level_hbm, level), (order_hbm, order))):
        cp = pltpu.make_async_copy(src, dst, small_sem.at[i])
        cp.start()
        small.append(cp)

    pm_copy = pltpu.make_async_copy(panels.at[:, :, :, pl.ds(0, MAIN)], pm, psem)
    pm_copy.start()
    pt_copies = []
    for r in range(R):
        cp = pltpu.make_async_copy(
            panels.at[:, r, :, pl.ds(MAIN, LAST)], pt.at[:, :, pl.ds(r * LAST, LAST)], ptsem.at[r]
        )
        cp.start()
        pt_copies.append(cp)
    own = pltpu.make_async_copy(shots.at[:, pl.ds(o * CH, CH)], recv1.at[pl.ds(2 * o, 2)], own_sem)
    own.start()

    out_ids = [((lax.rem(x + dx, 4) * 2 + lax.rem(yh + dy, 2)), a) for dx, dy in OUT_OFF]
    core_id = (o, (z * 2 + yl) * 2 + 1 - c)
    y_id = (o, (z * 2 + 1 - yl) * 2 + c)
    z_at = [lax.rem(z + dz, 8) for dz in Z_OFF]
    z_ids = [(o, (zz * 2 + yl) * 2 + c) for zz in z_at]

    barrier = pltpu.get_barrier_semaphore()
    peers = out_ids + [core_id, y_id] + z_ids
    for peer in peers:
        pl.semaphore_signal(barrier, inc=1, device_id=peer, device_id_type=MESH)
    pl.semaphore_wait(barrier, len(peers))

    first = []
    for i, peer in enumerate(out_ids):
        cp = pltpu.make_async_remote_copy(
            src_ref=shots.at[:, pl.ds(peer[0] * CH, CH)], dst_ref=recv1.at[pl.ds(2 * o, 2)],
            send_sem=s1.at[i], recv_sem=r1.at[i], device_id=peer, device_id_type=MESH,
        )
        cp.start()
        first.append(cp)

    for cp in small:
        cp.wait()

    def fill(l, _):
        for r in range(R):
            wt[l, :, r * LAST:(r + 1) * LAST] = jnp.full((1, LAST), table[l, r], F32)
        return 0

    lax.fori_loop(0, 8, fill, 0)
    pm_copy.wait()
    for cp in pt_copies:
        cp.wait()

    def weigh(k, _):
        lev = level[0, k]
        live = jnp.where(dest[0, k] >= 0, 1.0, 0.0).astype(F32)
        for r in range(R):
            tmp[r] = pm[k, r].astype(F32)
        tmpl[...] = pt[k].astype(F32)
        for r in range(R):
            weight = table[lev, r] * live
            re = tmp[r, 0:1] * weight
            im = tmp[r, 1:2] * weight
            pmf[k, 0, r] = re
            pmf[k, 1, r] = im - re
            pmf[k, 2, r] = re + im
        weight = wt[lev] * live
        re = tmpl[0:1] * weight
        im = tmpl[1:2] * weight
        for i, value in enumerate((re, im - re, re + im)):
            ptf[k, i] = value.reshape(R, LAST)
        return 0

    lax.fori_loop(0, K, weigh, 0)

    own.wait()
    for cp in first:
        cp.wait_recv()

    def remote(src, dst, send, recv, peer):
        cp = pltpu.make_async_remote_copy(
            src_ref=src, dst_ref=dst, send_sem=send, recv_sem=recv, device_id=peer, device_id_type=MESH
        )
        cp.start()
        return cp

    for s in range(S):
        gath[s, x, yh] = recv1[order[s]]

    def spread(s, peers, to, send, recv):
        part = gath.at[(s,) + to]
        return [remote(part, part, send.at[s, i], recv.at[s, i], peer) for i, peer in enumerate(peers)]

    second = [spread(s, out_ids, (x, yh), s2, r2) for s in range(S)]

    whole = (K, UNROLL, lambda i: i)

    def row(at):
        return (K // 2, UNROLL // 2, lambda i: (i // CH) * (2 * CH) + at * CH + lax.rem(i, CH))

    def traces(s, places, copies):
        for cp in copies:
            cp.wait_recv()
        count, _, location = places

        def body(i, _):
            k = location(i)
            tr[k] = gath[s, k // (2 * CH), (k // CH) % 2, k % CH].astype(F32)
            return 0

        lax.fori_loop(0, count, body, 0, unroll=4)

    def sums(places, load, cols, groups, shape):
        count, unroll, location = places

        def body(i, acc):
            k = location(i)
            a, b = tr[k, 0:1, cols], tr[k, 1:2, cols]
            t = (a + b, a, b)
            return tuple(acc[3 * g + n] + t[n] * load(k, n, g) for g in range(groups) for n in range(3))

        acc = lax.fori_loop(0, count, body, (jnp.zeros(shape, F32),) * (3 * groups), unroll=unroll)
        return [(acc[3 * g] - acc[3 * g + 2], acc[3 * g] + acc[3 * g + 1]) for g in range(groups)]

    def products(s, places, parts, more=False):
        for part in parts:
            if part < 4:
                pairs = sums(
                    places, lambda k, n, g, part=part: pmf[k, n, part * 8 + g], slice(0, MAIN), 8, (1, MAIN)
                )
                for g, pair in enumerate(pairs):
                    for n in range(2):
                        at = pl.ds(2 * (part * 8 + g) + n, 1)
                        xs[s, at] = xs[s, at] + pair[n] if more else pair[n]
            else:
                pairs = sums(
                    places, lambda k, n, g: ptf[k, n, g * 8:g * 8 + 8], slice(MAIN, F), 4, (8, LAST)
                )
                for g, pair in enumerate(pairs):
                    for n in range(2):
                        at = pl.ds(g * 16 + n, 8, stride=2)
                        xl[s, at] = xl[s, at] + pair[n] if more else pair[n]

    def turn(s):
        copies = []
        tiles = [xl[s] if ft == 8 else xs[s, :, ft * TILE:(ft + 1) * TILE] for ft in range(F // TILE)]
        turned = [pltpu.roll(tile, TILE // 2, 1) for tile in tiles[4:]]
        low = lax.broadcasted_iota(jnp.int32, (2 * R, TILE), 1) < TILE // 2
        for j in range(5):
            upper = jnp.where(low, turned[j], turned[min(j + 1, 4)])
            ts[j * TILE:(j + 1) * TILE] = jnp.concatenate([tiles[j], upper], axis=0).T
            if j in (2, 4):
                part = j // 4
                for b in range(part * 8, part * 8 + 8):
                    cs[s, b % 2, (b // 2) % 2, b // 4] = ts[b * FB:(b + 1) * FB]
                zz = pl.ds(2 * part, 2)
                copies.append(
                    remote(cs.at[s, 1 - c, :, zz], cr.at[s, :, zz], sc.at[s, part], rc.at[s, part], core_id)
                )
        return copies

    def y_start(s, copies):
        sent = []
        for part in range(2):
            copies[part].wait_recv()
            two = pl.ds(2 * part, 2)
            ys[s, two] = cs[s, c, 1 - yl, two] + cr[s, 1 - yl, two]
            sent.append(remote(ys.at[s, two], yr.at[s, two], sy.at[s, part], ry.at[s, part], y_id))
        yo[s] = cs[s, c, yl] + cr[s, yl]
        return sent

    def z_copy(s, to, slot):
        return pltpu.make_async_remote_copy(
            src_ref=zs.at[s, to], dst_ref=zr.at[s, slot], send_sem=sz.at[s, to], recv_sem=rz.at[s, slot],
            device_id=(o, (to * 2 + yl) * 2 + c), device_id_type=MESH,
        )

    def z_start(s, copies):
        low = lax.broadcasted_iota(jnp.int32, (HB, TILE), 1) < TILE // 2
        for part in range(2):
            copies[part].wait_recv()
            for zz in (2 * part, 2 * part + 1):
                first_half = yo[s, zz, 0:HB] + yr[s, zz, 0:HB]
                second_half = yo[s, zz, HB:FB] + yr[s, zz, HB:FB]
                zs[s, zz] = jnp.where(low, first_half, pltpu.roll(second_half, TILE // 2, 1))
                zs[s, zz + 4] = jnp.where(low, pltpu.roll(first_half, TILE // 2, 1), second_half)
            for to in (2 * part, 2 * part + 4, 2 * part + 1, 2 * part + 5):

                @pl.when(to != z)
                def _(to=to):
                    z_copy(s, to, z).start()

    def finish(s):
        for other in z_at:
            z_copy(s, other, other).wait_recv()
        total = zs[s, z]
        for other in z_at:
            total = total + zr[s, other]
        fs[s, 0:HB] = total
        flat = fs[s].T
        out[s, :, 0:HB] = flat[0:2 * R, 0:HB]
        out[s, :, HB:FB] = flat[2 * R:, 0:HB]

    own_row, other_row = row(yh), row(1 - yh)
    traces(0, own_row, second[0][3:6])
    products(0, own_row, range(5))
    traces(0, other_row, second[0][0:3] + second[0][6:7])
    products(0, other_row, range(5), more=True)
    core = [turn(0)]
    traces(1, whole, second[1])
    products(1, whole, range(3))
    y = [y_start(0, core[0])]
    products(1, whole, range(3, 5))
    core.append(turn(1))
    traces(2, whole, second[2])
    products(2, whole, range(3))
    y.append(y_start(1, core[1]))
    products(2, whole, range(3, 5))
    core.append(turn(2))
    traces(3, whole, second[3])
    products(3, whole, range(3))
    y.append(y_start(2, core[2]))
    z_start(0, y[0])
    products(3, whole, range(3, 5))
    core.append(turn(3))
    z_start(1, y[1])
    y.append(y_start(3, core[3]))
    z_start(2, y[2])
    z_start(3, y[3])
    for s in range(S):
        finish(s)

    for cp in first + [cp for copies in second + core + y for cp in copies]:
        cp.wait_send()
    for s in range(S):
        for other in z_at:
            z_copy(s, other, other).wait_send()


def on_device(panels, shot_data, taper_table, destination, taper_level, shot_order):
    vmem = pltpu.VMEM
    dma = pltpu.SemaphoreType.DMA
    hbm = pl.BlockSpec(memory_space=pltpu.HBM)
    result = pl.pallas_call(
        kernel,
        out_shape=jax.ShapeDtypeStruct((S, 2 * R, FB), F32),
        in_specs=[hbm] * 6,
        out_specs=pl.BlockSpec(memory_space=vmem),
        scratch_shapes=[
            pltpu.SMEM((8, R), F32),
            pltpu.SMEM((1, K), jnp.int32),
            pltpu.SMEM((1, K), jnp.int32),
            pltpu.SMEM((S,), jnp.int32),
            vmem((K, R, 2, MAIN), BF16),
            vmem((K, 2, R * LAST), BF16),
            vmem((R, 2, MAIN), F32),
            vmem((2, R * LAST), F32),
            vmem((K, 3, R, 1, MAIN), F32),
            vmem((K, 3, R, LAST), F32),
            vmem((8, 1, R * LAST), F32),
            vmem((2 * N_OUT, CH, 2, F), BF16),
            vmem((S, 4, 2, CH, 2, F), BF16),
            vmem((K, 2, F), F32),
            vmem((S, 2 * R, MAIN), F32),
            vmem((S, 2 * R, LAST), F32),
            vmem((5 * TILE, TILE), F32),
            vmem((S, 2, 2, 4, FB, TILE), F32),
            vmem((S, 2, 4, FB, TILE), F32),
            vmem((S, 4, FB, TILE), F32),
            vmem((S, 4, FB, TILE), F32),
            vmem((S, 4, FB, TILE), F32),
            vmem((S, 8, HB, TILE), F32),
            vmem((S, 8, HB, TILE), F32),
            vmem((S, TILE, TILE), F32),
            dma((4,)), dma, dma((R,)), dma,
            dma((7,)), dma((7,)), dma((S, 7)), dma((S, 7)),
            dma((S, 2)), dma((S, 2)), dma((S, 2)), dma((S, 2)), dma((S, 8)), dma((S, 8)),
        ],
        compiler_params=pltpu.CompilerParams(
            collective_id=0, has_side_effects=True, vmem_limit_bytes=48 * 2**20
        ),
        name="multiples",
    )(*[pltpu.with_memory_space_constraint(v, pltpu.HBM) for v in (panels, shot_data, taper_table, destination, taper_level, shot_order)])
    return result.reshape(S, R, 2, FB)


def solution(mesh):
    placed = (
        P("ap", "out", None, None),
        P("out", "ap", None, None),
        P(),
        P("out", "ap"),
        P("out", "ap"),
        P(),
    )
    return jax.shard_map(
        on_device, mesh=mesh, in_specs=placed, out_specs=P(None, "out", None, "ap"), check_vma=False
    )
```

```python
import functools

import jax
import jax.numpy as jnp
from jax import lax
from jax.experimental import pallas as pl
from jax.experimental.pallas import tpu as pltpu
from jax.sharding import PartitionSpec as P

F32 = jnp.float32
BF16 = jnp.bfloat16
MESH = pl.DeviceIdType.MESH

F = 1152
R = 32
K = 40
S = 4
N_OUT = 8
CH = K // N_OUT
TILE = 128
MAIN = 1024
LAST = F - MAIN
FB = 36
HB = FB // 2
UNROLL = 20

OUT_OFF = ((2, 1), (1, 1), (3, 1), (2, 0), (1, 0), (3, 0), (0, 1))
Z_OFF = (4, 3, 5, 2, 6, 1, 7)


def kernel(
    panels, shots, table_hbm, dest_hbm, level_hbm, order_hbm, out,
    table, dest, level, order,
    pm, pt, tmp, tmpl, pmf, ptf, wt, recv1, gath, tr, xs, xl, ts, cs, cr, ys, yo, yr, zs, zr, fs,
    small_sem, psem, ptsem, own_sem, s1, r1, s2, r2, sc, rc, sy, ry, sz, rz,
):
    o = lax.axis_index("out")
    a = lax.axis_index("ap")
    x, yh = o // 2, o % 2
    z, yl, c = a // 4, (a // 2) % 2, a % 2

    small = []
    for i, (src, dst) in enumerate(((table_hbm, table), (dest_hbm, dest), (level_hbm, level), (order_hbm, order))):
        cp = pltpu.make_async_copy(src, dst, small_sem.at[i])
        cp.start()
        small.append(cp)

    pm_copy = pltpu.make_async_copy(panels.at[:, :, :, pl.ds(0, MAIN)], pm, psem)
    pm_copy.start()
    pt_copies = []
    for r in range(R):
        cp = pltpu.make_async_copy(
            panels.at[:, r, :, pl.ds(MAIN, LAST)], pt.at[:, :, pl.ds(r * LAST, LAST)], ptsem.at[r]
        )
        cp.start()
        pt_copies.append(cp)
    own = pltpu.make_async_copy(shots.at[:, pl.ds(o * CH, CH)], recv1.at[pl.ds(2 * o, 2)], own_sem)
    own.start()

    out_ids = [((lax.rem(x + dx, 4) * 2 + lax.rem(yh + dy, 2)), a) for dx, dy in OUT_OFF]
    core_id = (o, (z * 2 + yl) * 2 + 1 - c)
    y_id = (o, (z * 2 + 1 - yl) * 2 + c)
    z_at = [lax.rem(z + dz, 8) for dz in Z_OFF]
    z_ids = [(o, (zz * 2 + yl) * 2 + c) for zz in z_at]

    barrier = pltpu.get_barrier_semaphore()
    peers = out_ids + [core_id, y_id] + z_ids
    for peer in peers:
        pl.semaphore_signal(barrier, inc=1, device_id=peer, device_id_type=MESH)
    pl.semaphore_wait(barrier, len(peers))

    first = []
    for i, peer in enumerate(out_ids):
        cp = pltpu.make_async_remote_copy(
            src_ref=shots.at[:, pl.ds(peer[0] * CH, CH)], dst_ref=recv1.at[pl.ds(2 * o, 2)],
            send_sem=s1.at[i], recv_sem=r1.at[i], device_id=peer, device_id_type=MESH,
        )
        cp.start()
        first.append(cp)

    for cp in small:
        cp.wait()

    def fill(l, _):
        for r in range(R):
            wt[l, :, r * LAST:(r + 1) * LAST] = jnp.full((1, LAST), table[l, r], F32)
        return 0

    lax.fori_loop(0, 8, fill, 0)
    pm_copy.wait()
    for cp in pt_copies:
        cp.wait()

    def weigh(k, _):
        lev = level[0, k]
        live = jnp.where(dest[0, k] >= 0, 1.0, 0.0).astype(F32)
        for r in range(R):
            tmp[r] = pm[k, r].astype(F32)
        tmpl[...] = pt[k].astype(F32)
        for r in range(R):
            weight = table[lev, r] * live
            re = tmp[r, 0:1] * weight
            im = tmp[r, 1:2] * weight
            pmf[k, 0, r] = re
            pmf[k, 1, r] = im - re
            pmf[k, 2, r] = re + im
        weight = wt[lev] * live
        re = tmpl[0:1] * weight
        im = tmpl[1:2] * weight
        for i, value in enumerate((re, im - re, re + im)):
            ptf[k, i] = value.reshape(R, LAST)
        return 0

    lax.fori_loop(0, K, weigh, 0)

    own.wait()
    for cp in first:
        cp.wait_recv()

    def remote(src, dst, send, recv, peer):
        cp = pltpu.make_async_remote_copy(
            src_ref=src, dst_ref=dst, send_sem=send, recv_sem=recv, device_id=peer, device_id_type=MESH
        )
        cp.start()
        return cp

    for s in range(S):
        gath[s, x, yh] = recv1[order[s]]

    def spread(s, peers, to, send, recv):
        part = gath.at[(s,) + to]
        return [remote(part, part, send.at[s, i], recv.at[s, i], peer) for i, peer in enumerate(peers)]

    second = [spread(s, out_ids, (x, yh), s2, r2) for s in range(S)]

    whole = (K, UNROLL, lambda i: i)

    def row(at):
        return (K // 2, UNROLL // 2, lambda i: (i // CH) * (2 * CH) + at * CH + lax.rem(i, CH))

    def traces(s, places, copies):
        for cp in copies:
            cp.wait_recv()
        count, _, location = places

        def body(i, _):
            k = location(i)
            tr[k] = gath[s, k // (2 * CH), (k // CH) % 2, k % CH].astype(F32)
            return 0

        lax.fori_loop(0, count, body, 0, unroll=4)

    def sums(places, load, cols, groups, shape):
        count, unroll, location = places

        def body(i, acc):
            k = location(i)
            a, b = tr[k, 0:1, cols], tr[k, 1:2, cols]
            t = (a + b, a, b)
            return tuple(acc[3 * g + n] + t[n] * load(k, n, g) for g in range(groups) for n in range(3))

        acc = lax.fori_loop(0, count, body, (jnp.zeros(shape, F32),) * (3 * groups), unroll=unroll)
        return [(acc[3 * g] - acc[3 * g + 2], acc[3 * g] + acc[3 * g + 1]) for g in range(groups)]

    def products(s, places, parts, more=False):
        for part in parts:
            if part < 4:
                pairs = sums(
                    places, lambda k, n, g, part=part: pmf[k, n, part * 8 + g], slice(0, MAIN), 8, (1, MAIN)
                )
                for g, pair in enumerate(pairs):
                    for n in range(2):
                        at = pl.ds(2 * (part * 8 + g) + n, 1)
                        xs[s, at] = xs[s, at] + pair[n] if more else pair[n]
            else:
                pairs = sums(
                    places, lambda k, n, g: ptf[k, n, g * 8:g * 8 + 8], slice(MAIN, F), 4, (8, LAST)
                )
                for g, pair in enumerate(pairs):
                    for n in range(2):
                        at = pl.ds(g * 16 + n, 8, stride=2)
                        xl[s, at] = xl[s, at] + pair[n] if more else pair[n]

    def turn(s):
        copies = []
        tiles = [xl[s] if ft == 8 else xs[s, :, ft * TILE:(ft + 1) * TILE] for ft in range(F // TILE)]
        turned = [pltpu.roll(tile, TILE // 2, 1) for tile in tiles[4:]]
        low = lax.broadcasted_iota(jnp.int32, (2 * R, TILE), 1) < TILE // 2
        for j in range(5):
            upper = jnp.where(low, turned[j], turned[min(j + 1, 4)])
            ts[j * TILE:(j + 1) * TILE] = jnp.concatenate([tiles[j], upper], axis=0).T
            if j in (2, 4):
                part = j // 4
                for b in range(part * 8, part * 8 + 8):
                    cs[s, b % 2, (b // 2) % 2, b // 4] = ts[b * FB:(b + 1) * FB]
                zz = pl.ds(2 * part, 2)
                copies.append(
                    remote(cs.at[s, 1 - c, :, zz], cr.at[s, :, zz], sc.at[s, part], rc.at[s, part], core_id)
                )
        return copies

    def y_start(s, copies):
        sent = []
        for part in range(2):
            copies[part].wait_recv()
            two = pl.ds(2 * part, 2)
            ys[s, two] = cs[s, c, 1 - yl, two] + cr[s, 1 - yl, two]
            sent.append(remote(ys.at[s, two], yr.at[s, two], sy.at[s, part], ry.at[s, part], y_id))
        yo[s] = cs[s, c, yl] + cr[s, yl]
        return sent

    def z_copy(s, to, slot):
        return pltpu.make_async_remote_copy(
            src_ref=zs.at[s, to], dst_ref=zr.at[s, slot], send_sem=sz.at[s, to], recv_sem=rz.at[s, slot],
            device_id=(o, (to * 2 + yl) * 2 + c), device_id_type=MESH,
        )

    def z_start(s, copies):
        low = lax.broadcasted_iota(jnp.int32, (HB, TILE), 1) < TILE // 2
        for part in range(2):
            copies[part].wait_recv()
            for zz in (2 * part, 2 * part + 1):
                first_half = yo[s, zz, 0:HB] + yr[s, zz, 0:HB]
                second_half = yo[s, zz, HB:FB] + yr[s, zz, HB:FB]
                zs[s, zz] = jnp.where(low, first_half, pltpu.roll(second_half, TILE // 2, 1))
                zs[s, zz + 4] = jnp.where(low, pltpu.roll(first_half, TILE // 2, 1), second_half)
            for to in (2 * part, 2 * part + 4, 2 * part + 1, 2 * part + 5):

                @pl.when(to != z)
                def _(to=to):
                    z_copy(s, to, z).start()

    def finish(s):
        for other in z_at:
            z_copy(s, other, other).wait_recv()
        total = zs[s, z]
        for other in z_at:
            total = total + zr[s, other]
        fs[s, 0:HB] = total
        flat = fs[s].T
        out[s, :, 0:HB] = flat[0:2 * R, 0:HB]
        out[s, :, HB:FB] = flat[2 * R:, 0:HB]

    own_row, other_row = row(yh), row(1 - yh)
    traces(0, own_row, second[0][3:6])
    products(0, own_row, range(5))
    traces(0, other_row, second[0][0:3] + second[0][6:7])
    products(0, other_row, range(5), more=True)
    core = [turn(0)]
    traces(1, whole, second[1])
    products(1, whole, range(4))
    y = [y_start(0, core[0])]
    products(1, whole, range(4, 5))
    core.append(turn(1))
    traces(2, whole, second[2])
    products(2, whole, range(4))
    y.append(y_start(1, core[1]))
    products(2, whole, range(4, 5))
    core.append(turn(2))
    traces(3, whole, second[3])
    products(3, whole, range(4))
    y.append(y_start(2, core[2]))
    z_start(0, y[0])
    products(3, whole, range(4, 5))
    core.append(turn(3))
    z_start(1, y[1])
    y.append(y_start(3, core[3]))
    z_start(2, y[2])
    z_start(3, y[3])
    for s in range(S):
        finish(s)

    for cp in first + [cp for copies in second + core + y for cp in copies]:
        cp.wait_send()
    for s in range(S):
        for other in z_at:
            z_copy(s, other, other).wait_send()


def on_device(panels, shot_data, taper_table, destination, taper_level, shot_order):
    vmem = pltpu.VMEM
    dma = pltpu.SemaphoreType.DMA
    hbm = pl.BlockSpec(memory_space=pltpu.HBM)
    result = pl.pallas_call(
        kernel,
        out_shape=jax.ShapeDtypeStruct((S, 2 * R, FB), F32),
        in_specs=[hbm] * 6,
        out_specs=pl.BlockSpec(memory_space=vmem),
        scratch_shapes=[
            pltpu.SMEM((8, R), F32),
            pltpu.SMEM((1, K), jnp.int32),
            pltpu.SMEM((1, K), jnp.int32),
            pltpu.SMEM((S,), jnp.int32),
            vmem((K, R, 2, MAIN), BF16),
            vmem((K, 2, R * LAST), BF16),
            vmem((R, 2, MAIN), F32),
            vmem((2, R * LAST), F32),
            vmem((K, 3, R, 1, MAIN), F32),
            vmem((K, 3, R, LAST), F32),
            vmem((8, 1, R * LAST), F32),
            vmem((2 * N_OUT, CH, 2, F), BF16),
            vmem((S, 4, 2, CH, 2, F), BF16),
            vmem((K, 2, F), F32),
            vmem((S, 2 * R, MAIN), F32),
            vmem((S, 2 * R, LAST), F32),
            vmem((5 * TILE, TILE), F32),
            vmem((S, 2, 2, 4, FB, TILE), F32),
            vmem((S, 2, 4, FB, TILE), F32),
            vmem((S, 4, FB, TILE), F32),
            vmem((S, 4, FB, TILE), F32),
            vmem((S, 4, FB, TILE), F32),
            vmem((S, 8, HB, TILE), F32),
            vmem((S, 8, HB, TILE), F32),
            vmem((S, TILE, TILE), F32),
            dma((4,)), dma, dma((R,)), dma,
            dma((7,)), dma((7,)), dma((S, 7)), dma((S, 7)),
            dma((S, 2)), dma((S, 2)), dma((S, 2)), dma((S, 2)), dma((S, 8)), dma((S, 8)),
        ],
        compiler_params=pltpu.CompilerParams(
            collective_id=0, has_side_effects=True, vmem_limit_bytes=48 * 2**20
        ),
        name="multiples",
    )(*[pltpu.with_memory_space_constraint(v, pltpu.HBM) for v in (panels, shot_data, taper_table, destination, taper_level, shot_order)])
    return result.reshape(S, R, 2, FB)


def solution(mesh):
    placed = (
        P("ap", "out", None, None),
        P("out", "ap", None, None),
        P(),
        P("out", "ap"),
        P("out", "ap"),
        P(),
    )
    return jax.shard_map(
        on_device, mesh=mesh, in_specs=placed, out_specs=P(None, "out", None, "ap"), check_vma=False
    )
```
